32 devices in a mesh: embed: 4 (over x, core), hidden: 8 (over z, y).
Axes of the slice: x: 2, y: 2, z: 4, core: 2. Of those that a mesh axis runs over, the one named last changes fastest.
Arguments:
- rows_in: bfloat16 [128, 16384], P('hidden', 'embed'), may hold values from -6 to 6
- gate_weight: bfloat16 [16384, 28672], P('embed', 'hidden'), may hold values from -0.046875 to 0.046875
- up_weight: bfloat16 [16384, 28672], P('embed', 'hidden'), may hold values from -0.046875 to 0.046875
- down_weight: bfloat16 [28672, 16384], P('hidden', 'embed'), may hold values from -0.03125 to 0.03125
Outputs:
- rows_out: bfloat16 [128, 16384], P('hidden', 'embed')
The draws below stay inside these ranges and needn't reach their ends.
All inputs are finite; a program needn't handle non-finite values.
Results may differ from the reference program's by a relative error of at most 0.0049.
Values may be sent and summed in bfloat16 or wider, within the bound.
A program may use at most 128 MiB of HBM per device.

```python
import jax
import jax.numpy as jnp

D = 16384
FFW = 28672
ROWS = 128


def shard_levels(rng, dims, split, low, largest):
    gain = 1.0
    for position, blocks in split:
        steps = jax.random.uniform(jax.random.fold_in(jax.random.fold_in(rng, 6), position), (blocks,), jnp.float32, low / len(split), largest / len(split))
        gain = gain * jnp.repeat(jnp.exp(steps), dims[position] // blocks).reshape((-1,) + (1,) * (len(dims) - 1 - position))
    return gain


def gaussian(own_key, shape, deviation, most, split=(), held_as=jnp.bfloat16):
    drawn = deviation * jax.random.normal(own_key, shape, jnp.float32)
    if split:
        drawn = drawn * shard_levels(own_key, shape, split, -0.22, 0.18)
    return jnp.clip(drawn, -most, most).astype(held_as)


def setup_inputs(seed: int = 0) -> dict:
    arg_keys = jax.random.split(jax.random.key(seed), 5)
    return {
        "rows_in": gaussian(arg_keys[0], (ROWS, D), 1.0, 6.0, ((0, 8), (1, 4))),
        "gate_weight": gaussian(arg_keys[1], (D, FFW), D ** -0.5, 0.046875, ((0, 4), (1, 8))),
        "up_weight": gaussian(arg_keys[2], (D, FFW), D ** -0.5, 0.046875, ((0, 4), (1, 8))),
        "down_weight": gaussian(arg_keys[3], (FFW, D), FFW ** -0.5, 0.03125, ((0, 8), (1, 4))),
    }


def reference(rows_in, gate_weight, up_weight, down_weight):
    gate = jnp.dot(rows_in, gate_weight, preferred_element_type=jnp.float32)
    up = jnp.dot(rows_in, up_weight, preferred_element_type=jnp.float32)
    act = (jax.nn.silu(gate) * up).astype(jnp.bfloat16)
    return jnp.dot(act, down_weight, preferred_element_type=jnp.float32).astype(jnp.bfloat16)
```

```python
import functools

import jax
import jax.numpy as jnp
from jax import lax
from jax.experimental import pallas as pl
from jax.experimental.pallas import tpu as pltpu
from jax.sharding import PartitionSpec as P

MESH = pl.DeviceIdType.MESH
F32 = jnp.float32
BF16 = jnp.bfloat16


def kernel(
    sizes, x_ref, gate_ref, up_ref, down_ref, out_ref,
    xg, wbuf, gu, l1r, l2s, l2r, act, yf, bs, br, zs, zr,
    wsem, own_sem, xa_s, xb_s, x_r, l1_ss, l1_rs, l2_ss, l2_rs,
    ax_ss, ax_rs, ac_ss, ac_rs, b_ss, b_rs, z_ss, z_rs,
):
    X, A, B, C, N, fc, S = sizes
    mine = x_ref.shape[0]
    rows, width = xg.shape
    hidden = act.shape[1]
    half = rows // 2
    rb = half // X
    e, h = lax.axis_index("embed"), lax.axis_index("hidden")
    x, c = e // 2, e % 2
    a, b = h // B, h % B
    half0 = pl.multiple_of(c * half, half)
    other0 = pl.multiple_of((1 - c) * half, half)
    own0 = pl.multiple_of(c * half + x * rb, rb)

    def at_embed(xx, cc):
        return {"embed": xx * 2 + cc, "hidden": h}

    def at_hidden(aa, bb):
        return {"embed": e, "hidden": aa * B + bb}

    def remote(src, dst, send, recv, where):
        return pltpu.make_async_remote_copy(
            src_ref=src, dst_ref=dst, send_sem=send, recv_sem=recv,
            device_id=where, device_id_type=MESH,
        )

    def cols(i):
        return pl.ds(pl.multiple_of(i * fc, fc), fc)

    def gate_tile(i, slot):
        return pltpu.make_async_copy(gate_ref.at[:, cols(i)], wbuf.at[slot, pl.ds(0, width), :], wsem.at[slot])

    def up_tile(i, slot):
        return pltpu.make_async_copy(up_ref.at[:, cols(i)], wbuf.at[slot, pl.ds(0, width), :], wsem.at[slot])

    def down_tile(j, slot):
        return pltpu.make_async_copy(down_ref.at[:, cols(j)], wbuf.at[slot, pl.ds(0, hidden), :], wsem.at[slot])

    for t in range(min(S, 2 * C)):
        (gate_tile if t % 2 == 0 else up_tile)(t // 2, t).start()

    def block(hh):
        return xg.at[pl.ds(pl.multiple_of(hh * mine, mine), mine), :]

    own = pltpu.make_async_copy(x_ref, block(h), own_sem)
    own.start()

    barrier = pltpu.get_barrier_semaphore()
    peers = [at_embed((x + k) % X, c) for k in range(1, X)] + [at_embed(x, 1 - c)]
    peers += [at_hidden((a + k) % A, b) for k in range(1, A)]
    peers += [at_hidden(a, (b + k) % B) for k in range(1, B)]
    for where in peers:
        pl.semaphore_signal(barrier, inc=1, device_id=where, device_id_type=MESH)
    pl.semaphore_wait(barrier, len(peers))

    def x_outer(k):
        return remote(x_ref, block(h), xa_s.at[k], x_r.at[h], at_hidden((a + k) % A, b))

    def x_inner(k, m):
        hh = ((a - k + A) % A) * B + b
        src = x_ref if k == 0 else block(hh)
        return remote(src, block(hh), xb_s.at[k, m], x_r.at[hh], at_hidden(a, (b + m) % B))

    def x_arrived(hh):
        remote(block(hh), block(hh), xa_s.at[0], x_r.at[hh], at_hidden(a, b)).wait_recv()

    for k in range(1, A):
        x_outer(k).start()
    for m in range(1, B):
        x_inner(0, m).start()
    for k in range(1, A):
        x_arrived(((a - k + A) % A) * B + b)
        for m in range(1, B):
            x_inner(k, m).start()
    own.wait()
    for k in range(A):
        for m in range(1, B):
            x_arrived(((a - k + A) % A) * B + (b + m) % B)

    def l1(i):
        return remote(
            gu.at[i, pl.ds(other0, half), :], l1r.at[i], l1_ss.at[i], l1_rs.at[i], at_embed(x, 1 - c))

    def l2(i, k):
        return remote(
            l2s.at[i, k - 1], l2r.at[i, k - 1], l2_ss.at[i, k - 1], l2_rs.at[i, k - 1],
            at_embed((x + k) % X, c))

    def ax(i, k):
        part = act.at[pl.ds(own0, rb), cols(i)]
        return remote(part, part, ax_ss.at[i, k - 1], ax_rs.at[i, k - 1], at_embed((x + k) % X, c))

    def ax_in(i, k):
        xx = (x - k + X) % X
        part = act.at[pl.ds(pl.multiple_of(c * half + xx * rb, rb), rb), cols(i)]
        return remote(part, part, ax_ss.at[i, k - 1], ax_rs.at[i, k - 1], at_embed(x, c))

    def ac(i):
        part = act.at[pl.ds(half0, half), cols(i)]
        return remote(part, part, ac_ss.at[i], ac_rs.at[i], at_embed(x, 1 - c))

    def ac_in(i):
        part = act.at[pl.ds(other0, half), cols(i)]
        return remote(part, part, ac_ss.at[i], ac_rs.at[i], at_embed(x, c))

    def hidden_step(i, _):
        @pl.when(i < C)
        def _():
            s0 = (2 * i) % S
            s1 = s0 + 1
            gate_tile(i, s0).wait()
            gu[i, :, pl.ds(0, fc)] = jnp.dot(
                xg[...], wbuf[s0, pl.ds(0, width), :], preferred_element_type=F32)
            up_tile(i, s1).wait()
            gu[i, :, pl.ds(fc, fc)] = jnp.dot(
                xg[...], wbuf[s1, pl.ds(0, width), :], preferred_element_type=F32)
            l1(i).start()
            t = 2 * i + S

            @pl.when(t < 2 * C)
            def _():
                gate_tile(t // 2, s0).start()
                up_tile(t // 2, s1).start()

            @pl.when((t >= 2 * C) & (t - 2 * C < N))
            def _():
                down_tile(t - 2 * C, s0).start()

            @pl.when((t >= 2 * C) & (t + 1 - 2 * C < N))
            def _():
                down_tile(t + 1 - 2 * C, s1).start()

        @pl.when((i >= 1) & (i < C + 1))
        def _():
            j = i - 1
            l1(j).wait_recv()
            for k in range(1, X):
                xx = (x + k) % X
                there = pl.ds(pl.multiple_of(xx * rb, rb), rb)
                here = pl.ds(pl.multiple_of(c * half + xx * rb, rb), rb)
                l2s[j, k - 1] = (gu[j, here, :] + l1r[j, there, :]).astype(BF16)
                l2(j, k).start()

        @pl.when((i >= 2) & (i < C + 2))
        def _():
            j = i - 2
            total = gu[j, pl.ds(own0, rb), :] + l1r[j, pl.ds(pl.multiple_of(x * rb, rb), rb), :]
            for k in range(1, X):
                l2(j, k).wait_recv()
                total = total + l2r[j, k - 1].astype(F32)
            g, u = total[:, :fc], total[:, fc:]
            act[pl.ds(own0, rb), cols(j)] = (g / (1.0 + jnp.exp(-g)) * u).astype(BF16)
            for k in range(1, X):
                ax(j, k).start()

        @pl.when(i >= 3)
        def _():
            j = i - 3
            for k in range(1, X):
                ax_in(j, k).wait_recv()
            ac(j).start()

        return 0

    lax.fori_loop(0, C + 3, hidden_step, 0)

    def act_in(i, _):
        ac_in(i).wait_recv()
        return 0

    lax.fori_loop(0, C, act_in, 0)

    def sb(j, m):
        return remote(
            bs.at[j, (b + m) % B], br.at[j, m - 1], b_ss.at[j, m - 1], b_rs.at[j, m - 1],
            at_hidden(a, (b + m) % B))

    def sz(j, k):
        return remote(
            zs.at[j, k - 1], zr.at[j, k - 1], z_ss.at[j, k - 1], z_rs.at[j, k - 1],
            at_hidden((a + k) % A, b))

    def inner_sum(j, aa):
        s = yf[j % 3, pl.ds(pl.multiple_of((aa * B + b) * mine, mine), mine), :]
        for m in range(1, B):
            s = s + br[j, m - 1, pl.ds(pl.multiple_of(aa * mine, mine), mine), :].astype(F32)
        return s

    def out_step(i, _):
        @pl.when(i < N)
        def _():
            t = 2 * C + i
            slot = t % S
            down_tile(i, slot).wait()
            yf[i % 3] = jnp.dot(act[...], wbuf[slot, pl.ds(0, hidden), :], preferred_element_type=F32)
            for aa in range(A):
                for bb in range(B):
                    bs[i, bb, pl.ds(aa * mine, mine), :] = yf[
                        i % 3, pl.ds((aa * B + bb) * mine, mine), :].astype(BF16)
            for m in range(1, B):
                sb(i, m).start()

            @pl.when(i + S < N)
            def _():
                down_tile(i + S, slot).start()

        @pl.when((i >= 1) & (i < N + 1))
        def _():
            j = i - 1
            for m in range(1, B):
                sb(j, m).wait_recv()
            for k in range(1, A):
                zs[j, k - 1] = inner_sum(j, (a + k) % A).astype(BF16)
                sz(j, k).start()

        @pl.when(i >= 2)
        def _():
            j = i - 2
            s = inner_sum(j, a)
            for k in range(1, A):
                sz(j, k).wait_recv()
                s = s + zr[j, k - 1].astype(F32)
            out_ref[:, cols(j)] = s.astype(BF16)

        return 0

    lax.fori_loop(0, N + 2, out_step, 0)

    for k in range(1, A):
        x_outer(k).wait_send()
    for k in range(A):
        for m in range(1, B):
            x_inner(k, m).wait_send()

    def hidden_sent(i, _):
        l1(i).wait_send()
        for k in range(1, X):
            l2(i, k).wait_send()
            ax(i, k).wait_send()
        ac(i).wait_send()
        return 0

    lax.fori_loop(0, C, hidden_sent, 0)

    def out_sent(j, _):
        for m in range(1, B):
            sb(j, m).wait_send()
        for k in range(1, A):
            sz(j, k).wait_send()
        return 0

    lax.fori_loop(0, N, out_sent, 0)


def on_device(embed, hidden_size, rows_in, gate_weight, up_weight, down_weight):
    mine, width = rows_in.shape
    hidden = gate_weight.shape[1]
    out_width = down_weight.shape[1]
    rows = mine * hidden_size
    X = embed // 2
    A = 4 if hidden_size % 4 == 0 else 1
    B = hidden_size // A
    C = 7
    fc = hidden // C
    N = out_width // fc
    S = 12
    dma = pltpu.SemaphoreType.DMA
    flops = 2 * rows * hidden * (2 * width + out_width)
    weights = 2 * hidden * (2 * width + out_width)
    half, rb = rows // 2, rows // embed
    return pl.pallas_call(
        functools.partial(kernel, (X, A, B, C, N, fc, S)),
        out_shape=jax.ShapeDtypeStruct((mine, out_width), BF16),
        in_specs=[pl.BlockSpec(memory_space=pl.ANY)] * 4,
        out_specs=pl.BlockSpec(memory_space=pltpu.VMEM),
        scratch_shapes=[
            pltpu.VMEM((rows, width), BF16),
            pltpu.VMEM((S, max(width, hidden), fc), BF16),
            pltpu.VMEM((C, rows, 2 * fc), F32),
            pltpu.VMEM((C, half, 2 * fc), F32),
            pltpu.VMEM((C, X - 1, rb, 2 * fc), BF16),
            pltpu.VMEM((C, X - 1, rb, 2 * fc), BF16),
            pltpu.VMEM((rows, hidden), BF16),
            pltpu.VMEM((3, rows, fc), F32),
            pltpu.VMEM((N, B, A * mine, fc), BF16),
            pltpu.VMEM((N, B - 1, A * mine, fc), BF16),
            pltpu.VMEM((N, A - 1, mine, fc), BF16),
            pltpu.VMEM((N, A - 1, mine, fc), BF16),
            dma((S,)), dma(()), dma((A,)), dma((A, B)), dma((hidden_size,)),
            dma((C,)), dma((C,)), dma((C, X - 1)), dma((C, X - 1)),
            dma((C, X - 1)), dma((C, X - 1)), dma((C,)), dma((C,)),
            dma((N, B - 1)), dma((N, B - 1)), dma((N, A - 1)), dma((N, A - 1)),
        ],
        compiler_params=pltpu.CompilerParams(
            collective_id=0, has_side_effects=True, vmem_limit_bytes=63 * 2**20
        ),
        cost_estimate=pl.CostEstimate(
            flops=flops, bytes_accessed=weights, transcendentals=rows * hidden // embed),
    )(rows_in, gate_weight, up_weight, down_weight)


def solution(mesh):
    placed = (
        P("hidden", "embed"),
        P("embed", "hidden"),
        P("embed", "hidden"),
        P("hidden", "embed"),
    )
    body = functools.partial(on_device, mesh.shape["embed"], mesh.shape["hidden"])
    return jax.shard_map(
        body, mesh=mesh, in_specs=placed, out_specs=P("hidden", "embed"), check_vma=False
    )
```

```python
import functools

import jax
import jax.numpy as jnp
from jax import lax
from jax.experimental import pallas as pl
from jax.experimental.pallas import tpu as pltpu
from jax.sharding import PartitionSpec as P

MESH = pl.DeviceIdType.MESH
F32 = jnp.float32
BF16 = jnp.bfloat16


def kernel(
    sizes, x_ref, gate_ref, up_ref, down_ref, out_ref,
    xg, wbuf, gu, l1r, l2s, l2r, act, yf, bs, br, zs, zr,
    wsem, own_sem, xa_s, xb_s, x_r, l1_ss, l1_rs, l2_ss, l2_rs,
    ax_ss, ax_rs, ac_ss, ac_rs, b_ss, b_rs, z_ss, z_rs,
):
    X, A, B, C, N, fc, S, G, E, D = sizes
    mine = x_ref.shape[0]
    rows, width = xg.shape
    hidden = act.shape[1]
    half = rows // 2
    rb = half // X
    e, h = lax.axis_index("embed"), lax.axis_index("hidden")
    x, c = e // 2, e % 2
    a, b = h // B, h % B
    half0 = pl.multiple_of(c * half, half)
    other0 = pl.multiple_of((1 - c) * half, half)
    own0 = pl.multiple_of(c * half + x * rb, rb)

    def at_embed(xx, cc):
        return {"embed": xx * 2 + cc, "hidden": h}

    def at_hidden(aa, bb):
        return {"embed": e, "hidden": aa * B + bb}

    def remote(src, dst, send, recv, where):
        return pltpu.make_async_remote_copy(
            src_ref=src, dst_ref=dst, send_sem=send, recv_sem=recv,
            device_id=where, device_id_type=MESH,
        )

    def cols(i):
        return pl.ds(pl.multiple_of(i * fc, fc), fc)

    def gate_tile(i, slot):
        return pltpu.make_async_copy(gate_ref.at[:, cols(i)], wbuf.at[slot, pl.ds(0, width), :], wsem.at[slot])

    def up_tile(i, slot):
        return pltpu.make_async_copy(up_ref.at[:, cols(i)], wbuf.at[slot, pl.ds(0, width), :], wsem.at[slot])

    def down_tile(j, slot):
        return pltpu.make_async_copy(down_ref.at[:, cols(j)], wbuf.at[slot, pl.ds(0, hidden), :], wsem.at[slot])

    for t in range(min(S, 2 * C)):
        (gate_tile if t % 2 == 0 else up_tile)(t // 2, t).start()

    def block(hh):
        return xg.at[pl.ds(pl.multiple_of(hh * mine, mine), mine), :]

    own = pltpu.make_async_copy(x_ref, block(h), own_sem)
    own.start()

    barrier = pltpu.get_barrier_semaphore()
    peers = [at_embed((x + k) % X, c) for k in range(1, X)] + [at_embed(x, 1 - c)]
    peers += [at_hidden((a + k) % A, b) for k in range(1, A)]
    peers += [at_hidden(a, (b + k) % B) for k in range(1, B)]
    for where in peers:
        pl.semaphore_signal(barrier, inc=1, device_id=where, device_id_type=MESH)
    pl.semaphore_wait(barrier, len(peers))

    part = width // 2

    def piece(ref, q):
        return ref.at[:, pl.ds(q * part, part)]

    def x_outer(k, q):
        return remote(
            piece(x_ref, q), piece(block(h), q), xa_s.at[q, k], x_r.at[q, h], at_hidden((a + k) % A, b))

    def x_inner(k, m, q):
        hh = ((a - k + A) % A) * B + b
        src = block(hh) if not isinstance(k, int) or k > 0 else x_ref
        return remote(
            piece(src, q), piece(block(hh), q), xb_s.at[q, k, m], x_r.at[q, hh], at_hidden(a, (b + m) % B))

    def x_arrived(hh, q):
        there = piece(block(hh), q)
        remote(there, there, xa_s.at[q, 0], x_r.at[q, hh], at_hidden(a, b)).wait_recv()

    def x_forward(k, q):
        x_arrived(((a - k + A) % A) * B + b, q)
        for m in range(1, B):
            x_inner(k, m, q).start()

    def x_rest(q):
        for k in range(A):
            for m in range(1, B):
                x_arrived(((a - k + A) % A) * B + (b + m) % B, q)

    for q in range(2):
        for k in range(1, A):
            x_outer(k, q).start()
        for m in range(1, B):
            x_inner(0, m, q).start()
    for k in range(1, A):
        x_forward(k, 0)
    own.wait()
    x_rest(0)

    def early_step(i, _):
        for n, tile in ((0, gate_tile), (1, up_tile)):
            tile(i, 2 * i + n).wait()
            gu[i, :, pl.ds(n * fc, fc)] = jnp.dot(
                xg[:, pl.ds(0, part)], wbuf[2 * i + n, pl.ds(0, part), :], preferred_element_type=F32)

        @pl.when(i < A - 1)
        def _():
            x_forward(i + 1, 1)

        return 0

    lax.fori_loop(0, G, early_step, 0)
    x_rest(1)

    def l1(i):
        return remote(
            gu.at[i, pl.ds(other0, half), :], l1r.at[i], l1_ss.at[i], l1_rs.at[i], at_embed(x, 1 - c))

    def l2(i, k):
        return remote(
            l2s.at[i, k - 1], l2r.at[i, k - 1], l2_ss.at[i, k - 1], l2_rs.at[i, k - 1],
            at_embed((x + k) % X, c))

    def ax(i, k):
        part = act.at[pl.ds(own0, rb), cols(i)]
        return remote(part, part, ax_ss.at[i, k - 1], ax_rs.at[i, k - 1], at_embed((x + k) % X, c))

    def ax_in(i, k):
        xx = (x - k + X) % X
        part = act.at[pl.ds(pl.multiple_of(c * half + xx * rb, rb), rb), cols(i)]
        return remote(part, part, ax_ss.at[i, k - 1], ax_rs.at[i, k - 1], at_embed(x, c))

    def ac(i):
        part = act.at[pl.ds(half0, half), cols(i)]
        return remote(part, part, ac_ss.at[i], ac_rs.at[i], at_embed(x, 1 - c))

    def ac_in(i):
        part = act.at[pl.ds(other0, half), cols(i)]
        return remote(part, part, ac_ss.at[i], ac_rs.at[i], at_embed(x, c))

    def hidden_step(i, _):
        @pl.when(i < G)
        def _():
            for n in range(2):
                gu[i, :, pl.ds(n * fc, fc)] += jnp.dot(
                    xg[:, pl.ds(part, part)], wbuf[(2 * i + n) % S, pl.ds(part, part), :],
                    preferred_element_type=F32)

        @pl.when((i >= G) & (i < C))
        def _():
            for n, tile in ((0, gate_tile), (1, up_tile)):
                slot = (2 * i + n) % S
                tile(i, slot).wait()
                gu[i, :, pl.ds(n * fc, fc)] = jnp.dot(
                    xg[...], wbuf[slot, pl.ds(0, width), :], preferred_element_type=F32)

        @pl.when(i < C)
        def _():
            s0 = (2 * i) % S
            s1 = s0 + 1
            l1(i).start()
            t = 2 * i + S

            @pl.when(t < 2 * C)
            def _():
                gate_tile(t // 2, s0).start()
                up_tile(t // 2, s1).start()

            @pl.when((t >= 2 * C) & (t - 2 * C < N))
            def _():
                down_tile(t - 2 * C, s0).start()

            @pl.when((t >= 2 * C) & (t + 1 - 2 * C < N))
            def _():
                down_tile(t + 1 - 2 * C, s1).start()

        @pl.when(i == C)
        def _():
            for j in range(E):
                ac_in(j).wait_recv()

        @pl.when(i >= C)
        def _():
            for n in range(D // 3):
                j = (i - C) * (D // 3) + n
                slot = (2 * C + j) % S
                down_tile(j, slot).wait()
                yf[j] = jnp.dot(
                    act[:, pl.ds(0, E * fc)], wbuf[slot, pl.ds(0, E * fc), :], preferred_element_type=F32)

        @pl.when((i >= 1) & (i < C + 1))
        def _():
            j = i - 1
            l1(j).wait_recv()
            for k in range(1, X):
                xx = (x + k) % X
                there = pl.ds(pl.multiple_of(xx * rb, rb), rb)
                here = pl.ds(pl.multiple_of(c * half + xx * rb, rb), rb)
                l2s[j, k - 1] = (gu[j, here, :] + l1r[j, there, :]).astype(BF16)
                l2(j, k).start()

        @pl.when((i >= 2) & (i < C + 2))
        def _():
            j = i - 2
            total = gu[j, pl.ds(own0, rb), :] + l1r[j, pl.ds(pl.multiple_of(x * rb, rb), rb), :]
            for k in range(1, X):
                l2(j, k).wait_recv()
                total = total + l2r[j, k - 1].astype(F32)
            g, u = total[:, :fc], total[:, fc:]
            act[pl.ds(own0, rb), cols(j)] = (g / (1.0 + jnp.exp(-g)) * u).astype(BF16)
            for k in range(1, X):
                ax(j, k).start()

        @pl.when(i >= 3)
        def _():
            j = i - 3
            for k in range(1, X):
                ax_in(j, k).wait_recv()
            ac(j).start()

        return 0

    lax.fori_loop(0, C + 3, hidden_step, 0)

    def act_in(i, _):
        ac_in(i).wait_recv()
        return 0

    lax.fori_loop(E, C, act_in, 0)

    def sb(j, m):
        return remote(
            bs.at[j, (b + m) % B], br.at[j, m - 1], b_ss.at[j, m - 1], b_rs.at[j, m - 1],
            at_hidden(a, (b + m) % B))

    def sz(j, k):
        return remote(
            zs.at[j, k - 1], zr.at[j, k - 1], z_ss.at[j, k - 1], z_rs.at[j, k - 1],
            at_hidden((a + k) % A, b))

    def inner_sum(j, aa):
        s = yf[j, pl.ds(pl.multiple_of((aa * B + b) * mine, mine), mine), :]
        for m in range(1, B):
            s = s + br[j, m - 1, pl.ds(pl.multiple_of(aa * mine, mine), mine), :].astype(F32)
        return s

    def out_step(i, _):
        slot = (2 * C + i) % S
        late = pl.ds(E * fc, hidden - E * fc)

        @pl.when(i < D)
        def _():
            yf[i] += jnp.dot(act[:, late], wbuf[slot, late, :], preferred_element_type=F32)

        @pl.when((i >= D) & (i < N))
        def _():
            down_tile(i, slot).wait()
            yf[i] = jnp.dot(act[...], wbuf[slot, pl.ds(0, hidden), :], preferred_element_type=F32)

        @pl.when(i < N)
        def _():
            for aa in range(A):
                for bb in range(B):
                    bs[i, bb, pl.ds(aa * mine, mine), :] = yf[
                        i, pl.ds((aa * B + bb) * mine, mine), :].astype(BF16)
            for m in range(1, B):
                sb(i, m).start()

            @pl.when(i + S < N)
            def _():
                down_tile(i + S, slot).start()

        @pl.when((i >= 1) & (i < N + 1))
        def _():
            j = i - 1
            for m in range(1, B):
                sb(j, m).wait_recv()
            for k in range(1, A):
                zs[j, k - 1] = inner_sum(j, (a + k) % A).astype(BF16)
                sz(j, k).start()

        @pl.when(i >= 2)
        def _():
            j = i - 2
            s = inner_sum(j, a)
            for k in range(1, A):
                sz(j, k).wait_recv()
                s = s + zr[j, k - 1].astype(F32)
            out_ref[:, cols(j)] = s.astype(BF16)

        return 0

    lax.fori_loop(0, N + 2, out_step, 0)

    for q in range(2):
        for k in range(1, A):
            x_outer(k, q).wait_send()
        for k in range(A):
            for m in range(1, B):
                x_inner(k, m, q).wait_send()

    def hidden_sent(i, _):
        l1(i).wait_send()
        for k in range(1, X):
            l2(i, k).wait_send()
            ax(i, k).wait_send()
        ac(i).wait_send()
        return 0

    lax.fori_loop(0, C, hidden_sent, 0)

    def out_sent(j, _):
        for m in range(1, B):
            sb(j, m).wait_send()
        for k in range(1, A):
            sz(j, k).wait_send()
        return 0

    lax.fori_loop(0, N, out_sent, 0)


def on_device(embed, hidden_size, rows_in, gate_weight, up_weight, down_weight):
    mine, width = rows_in.shape
    hidden = gate_weight.shape[1]
    out_width = down_weight.shape[1]
    rows = mine * hidden_size
    X = embed // 2
    A = 4 if hidden_size % 4 == 0 else 1
    B = hidden_size // A
    C = 7
    fc = hidden // C
    N = out_width // fc
    S, G, E, D = 12, 4, C - 3, 6
    dma = pltpu.SemaphoreType.DMA
    flops = 2 * rows * hidden * (2 * width + out_width)
    weights = 2 * hidden * (2 * width + out_width)
    half, rb = rows // 2, rows // embed
    return pl.pallas_call(
        functools.partial(kernel, (X, A, B, C, N, fc, S, G, E, D)),
        out_shape=jax.ShapeDtypeStruct((mine, out_width), BF16),
        in_specs=[pl.BlockSpec(memory_space=pl.ANY)] * 4,
        out_specs=pl.BlockSpec(memory_space=pltpu.VMEM),
        scratch_shapes=[
            pltpu.VMEM((rows, width), BF16),
            pltpu.VMEM((S, max(width, hidden), fc), BF16),
            pltpu.VMEM((C, rows, 2 * fc), F32),
            pltpu.VMEM((C, half, 2 * fc), F32),
            pltpu.VMEM((C, X - 1, rb, 2 * fc), BF16),
            pltpu.VMEM((C, X - 1, rb, 2 * fc), BF16),
            pltpu.VMEM((rows, hidden), BF16),
            pltpu.VMEM((N, rows, fc), F32),
            pltpu.VMEM((N, B, A * mine, fc), BF16),
            pltpu.VMEM((N, B - 1, A * mine, fc), BF16),
            pltpu.VMEM((N, A - 1, mine, fc), BF16),
            pltpu.VMEM((N, A - 1, mine, fc), BF16),
            dma((S,)), dma(()), dma((2, A)), dma((2, A, B)), dma((2, hidden_size)),
            dma((C,)), dma((C,)), dma((C, X - 1)), dma((C, X - 1)),
            dma((C, X - 1)), dma((C, X - 1)), dma((C,)), dma((C,)),
            dma((N, B - 1)), dma((N, B - 1)), dma((N, A - 1)), dma((N, A - 1)),
        ],
        compiler_params=pltpu.CompilerParams(
            collective_id=0, has_side_effects=True, vmem_limit_bytes=63 * 2**20
        ),
        cost_estimate=pl.CostEstimate(
            flops=flops, bytes_accessed=weights, transcendentals=rows * hidden // embed),
    )(rows_in, gate_weight, up_weight, down_weight)


def solution(mesh):
    placed = (
        P("hidden", "embed"),
        P("embed", "hidden"),
        P("embed", "hidden"),
        P("hidden", "embed"),
    )
    body = functools.partial(on_device, mesh.shape["embed"], mesh.shape["hidden"])
    return jax.shard_map(
        body, mesh=mesh, in_specs=placed, out_specs=P("hidden", "embed"), check_vma=False
    )
```

```python
import functools

import jax
import jax.numpy as jnp
from jax import lax
from jax.experimental import pallas as pl
from jax.experimental.pallas import tpu as pltpu
from jax.sharding import PartitionSpec as P

MESH = pl.DeviceIdType.MESH
F32 = jnp.float32
BF16 = jnp.bfloat16


def kernel(
    sizes, x_ref, gate_ref, up_ref, down_ref, out_ref,
    xg, wbuf, gu, l1r, l2s, l2r, act, yf, bs, br, zs, zr,
    wsem, own_sem, xa_s, xb_s, x_r, l1_ss, l1_rs, l2_ss, l2_rs,
    ax_ss, ax_rs, ac_ss, ac_rs, b_ss, b_rs, z_ss, z_rs,
):
    X, A, B, C, N, fc, S, G, E, D = sizes
    mine = x_ref.shape[0]
    rows, width = xg.shape
    hidden = act.shape[1]
    half = rows // 2
    rb = half // X
    e, h = lax.axis_index("embed"), lax.axis_index("hidden")
    x, c = e // 2, e % 2
    a, b = h // B, h % B
    half0 = pl.multiple_of(c * half, half)
    other0 = pl.multiple_of((1 - c) * half, half)
    own0 = pl.multiple_of(c * half + x * rb, rb)

    def at_embed(xx, cc):
        return {"embed": xx * 2 + cc, "hidden": h}

    def at_hidden(aa, bb):
        return {"embed": e, "hidden": aa * B + bb}

    def remote(src, dst, send, recv, where):
        return pltpu.make_async_remote_copy(
            src_ref=src, dst_ref=dst, send_sem=send, recv_sem=recv,
            device_id=where, device_id_type=MESH,
        )

    def cols(i):
        return pl.ds(pl.multiple_of(i * fc, fc), fc)

    def gate_tile(i, slot):
        return pltpu.make_async_copy(gate_ref.at[:, cols(i)], wbuf.at[slot, pl.ds(0, width), :], wsem.at[slot])

    def up_tile(i, slot):
        return pltpu.make_async_copy(up_ref.at[:, cols(i)], wbuf.at[slot, pl.ds(0, width), :], wsem.at[slot])

    def down_tile(j, slot):
        return pltpu.make_async_copy(down_ref.at[:, cols(j)], wbuf.at[slot, pl.ds(0, hidden), :], wsem.at[slot])

    def first_tiles(begin, end):
        for t in range(begin, end):
            (gate_tile if t % 2 == 0 else up_tile)(t // 2, t).start()

    first_tiles(0, 4)

    def block(hh):
        return xg.at[pl.ds(pl.multiple_of(hh * mine, mine), mine), :]

    own = pltpu.make_async_copy(x_ref, block(h), own_sem)
    own.start()

    barrier = pltpu.get_barrier_semaphore()
    peers = [at_embed((x + k) % X, c) for k in range(1, X)] + [at_embed(x, 1 - c)]
    peers += [at_hidden((a + k) % A, b) for k in range(1, A)]
    peers += [at_hidden(a, (b + k) % B) for k in range(1, B)]
    for where in peers:
        pl.semaphore_signal(barrier, inc=1, device_id=where, device_id_type=MESH)
    pl.semaphore_wait(barrier, len(peers))

    part = width // 2

    def piece(ref, q):
        return ref.at[:, pl.ds(q * part, part)]

    def x_outer(k, q):
        return remote(
            piece(x_ref, q), piece(block(h), q), xa_s.at[q, k], x_r.at[q, h], at_hidden((a + k) % A, b))

    def x_inner(k, m, q):
        hh = ((a - k + A) % A) * B + b
        src = block(hh) if not isinstance(k, int) or k > 0 else x_ref
        return remote(
            piece(src, q), piece(block(hh), q), xb_s.at[q, k, m], x_r.at[q, hh], at_hidden(a, (b + m) % B))

    def x_arrived(hh, q):
        there = piece(block(hh), q)
        remote(there, there, xa_s.at[q, 0], x_r.at[q, hh], at_hidden(a, b)).wait_recv()

    def x_forward(k, q):
        x_arrived(((a - k + A) % A) * B + b, q)
        for m in range(1, B):
            x_inner(k, m, q).start()

    def x_rest(q):
        for k in range(A):
            for m in range(1, B):
                x_arrived(((a - k + A) % A) * B + (b + m) % B, q)

    for q in range(2):
        for k in range(1, A):
            x_outer(k, q).start()
        for m in range(1, B):
            x_inner(0, m, q).start()
    first_tiles(4, S)
    for k in range(1, A):
        x_forward(k, 0)
    own.wait()
    x_rest(0)

    def early_step(i, _):
        for n, tile in ((0, gate_tile), (1, up_tile)):
            tile(i, 2 * i + n).wait()
            gu[i, :, pl.ds(n * fc, fc)] = jnp.dot(
                xg[:, pl.ds(0, part)], wbuf[2 * i + n, pl.ds(0, part), :], preferred_element_type=F32)

        @pl.when(i < A - 1)
        def _():
            x_forward(i + 1, 1)

        return 0

    lax.fori_loop(0, G, early_step, 0)
    x_rest(1)

    def l1(i):
        return remote(
            gu.at[i, pl.ds(other0, half), :], l1r.at[i], l1_ss.at[i], l1_rs.at[i], at_embed(x, 1 - c))

    def l2(i, k):
        return remote(
            l2s.at[i, k - 1], l2r.at[i, k - 1], l2_ss.at[i, k - 1], l2_rs.at[i, k - 1],
            at_embed((x + k) % X, c))

    def ax(i, k):
        part = act.at[pl.ds(own0, rb), cols(i)]
        return remote(part, part, ax_ss.at[i, k - 1], ax_rs.at[i, k - 1], at_embed((x + k) % X, c))

    def ax_in(i, k):
        xx = (x - k + X) % X
        part = act.at[pl.ds(pl.multiple_of(c * half + xx * rb, rb), rb), cols(i)]
        return remote(part, part, ax_ss.at[i, k - 1], ax_rs.at[i, k - 1], at_embed(x, c))

    def ac(i):
        part = act.at[pl.ds(half0, half), cols(i)]
        return remote(part, part, ac_ss.at[i], ac_rs.at[i], at_embed(x, 1 - c))

    def ac_in(i):
        part = act.at[pl.ds(other0, half), cols(i)]
        return remote(part, part, ac_ss.at[i], ac_rs.at[i], at_embed(x, c))

    def hidden_step(i, _):
        @pl.when(i < G)
        def _():
            for n in range(2):
                gu[i, :, pl.ds(n * fc, fc)] += jnp.dot(
                    xg[:, pl.ds(part, part)], wbuf[(2 * i + n) % S, pl.ds(part, part), :],
                    preferred_element_type=F32)

        @pl.when((i >= G) & (i < C))
        def _():
            for n, tile in ((0, gate_tile), (1, up_tile)):
                slot = (2 * i + n) % S
                tile(i, slot).wait()
                gu[i, :, pl.ds(n * fc, fc)] = jnp.dot(
                    xg[...], wbuf[slot, pl.ds(0, width), :], preferred_element_type=F32)

        @pl.when(i < C)
        def _():
            s0 = (2 * i) % S
            s1 = s0 + 1
            l1(i).start()
            t = 2 * i + S

            @pl.when(t < 2 * C)
            def _():
                gate_tile(t // 2, s0).start()
                up_tile(t // 2, s1).start()

            @pl.when((t >= 2 * C) & (t - 2 * C < N))
            def _():
                down_tile(t - 2 * C, s0).start()

            @pl.when((t >= 2 * C) & (t + 1 - 2 * C < N))
            def _():
                down_tile(t + 1 - 2 * C, s1).start()

        @pl.when((i >= 1) & (i < C + 1))
        def _():
            j = i - 1
            l1(j).wait_recv()
            for k in range(1, X):
                xx = (x + k) % X
                there = pl.ds(pl.multiple_of(xx * rb, rb), rb)
                here = pl.ds(pl.multiple_of(c * half + xx * rb, rb), rb)
                l2s[j, k - 1] = (gu[j, here, :] + l1r[j, there, :]).astype(BF16)
                l2(j, k).start()

        @pl.when((i >= 2) & (i < C + 2))
        def _():
            j = i - 2
            total = gu[j, pl.ds(own0, rb), :] + l1r[j, pl.ds(pl.multiple_of(x * rb, rb), rb), :]
            for k in range(1, X):
                l2(j, k).wait_recv()
                total = total + l2r[j, k - 1].astype(F32)
            g, u = total[:, :fc], total[:, fc:]
            act[pl.ds(own0, rb), cols(j)] = (g / (1.0 + jnp.exp(-g)) * u).astype(BF16)
            for k in range(1, X):
                ax(j, k).start()

        @pl.when(i >= 3)
        def _():
            j = i - 3
            for k in range(1, X):
                ax_in(j, k).wait_recv()
            ac(j).start()

        @pl.when(i == C)
        def _():
            for j in range(E):
                ac_in(j).wait_recv()

        @pl.when(i >= C)
        def _():
            j = i - C
            slot = (2 * C + j) % S
            down_tile(j, slot).wait()
            yf[j] = jnp.dot(
                act[:, pl.ds(0, E * fc)], wbuf[slot, pl.ds(0, E * fc), :], preferred_element_type=F32)

        return 0

    lax.fori_loop(0, C + 3, hidden_step, 0)

    def act_in(i, _):
        ac_in(i).wait_recv()
        return 0

    lax.fori_loop(E, C, act_in, 0)

    def sb(j, m):
        return remote(
            bs.at[j, (b + m) % B], br.at[j, m - 1], b_ss.at[j, m - 1], b_rs.at[j, m - 1],
            at_hidden(a, (b + m) % B))

    def sz(j, k):
        return remote(
            zs.at[j, k - 1], zr.at[j, k - 1], z_ss.at[j, k - 1], z_rs.at[j, k - 1],
            at_hidden((a + k) % A, b))

    def inner_sum(j, aa):
        s = yf[j, pl.ds(pl.multiple_of((aa * B + b) * mine, mine), mine), :]
        for m in range(1, B):
            s = s + br[j, m - 1, pl.ds(pl.multiple_of(aa * mine, mine), mine), :].astype(F32)
        return s

    def out_step(i, _):
        slot = (2 * C + i) % S
        late = pl.ds(E * fc, hidden - E * fc)

        @pl.when(i < D)
        def _():
            yf[i] += jnp.dot(act[:, late], wbuf[slot, late, :], preferred_element_type=F32)

        @pl.when((i >= D) & (i < N))
        def _():
            down_tile(i, slot).wait()
            yf[i] = jnp.dot(act[...], wbuf[slot, pl.ds(0, hidden), :], preferred_element_type=F32)

        @pl.when(i < N)
        def _():
            for aa in range(A):
                for bb in range(B):
                    bs[i, bb, pl.ds(aa * mine, mine), :] = yf[
                        i, pl.ds((aa * B + bb) * mine, mine), :].astype(BF16)
            for m in range(1, B):
                sb(i, m).start()

            @pl.when(i + S < N)
            def _():
                down_tile(i + S, slot).start()

        @pl.when((i >= 2) & (i < N + 2))
        def _():
            j = i - 2
            for m in range(1, B):
                sb(j, m).wait_recv()
            for k in range(1, A):
                zs[j, k - 1] = inner_sum(j, (a + k) % A).astype(BF16)
                sz(j, k).start()

        @pl.when(i >= 4)
        def _():
            j = i - 4
            s = inner_sum(j, a)
            for k in range(1, A):
                sz(j, k).wait_recv()
                s = s + zr[j, k - 1].astype(F32)
            out_ref[:, cols(j)] = s.astype(BF16)

        return 0

    lax.fori_loop(0, N + 4, out_step, 0)

    for q in range(2):
        for k in range(1, A):
            x_outer(k, q).wait_send()
        for k in range(A):
            for m in range(1, B):
                x_inner(k, m, q).wait_send()

    def hidden_sent(i, _):
        l1(i).wait_send()
        for k in range(1, X):
            l2(i, k).wait_send()
            ax(i, k).wait_send()
        ac(i).wait_send()
        return 0

    lax.fori_loop(0, C, hidden_sent, 0)

    def out_sent(j, _):
        for m in range(1, B):
            sb(j, m).wait_send()
        for k in range(1, A):
            sz(j, k).wait_send()
        return 0

    lax.fori_loop(0, N, out_sent, 0)


def on_device(embed, hidden_size, rows_in, gate_weight, up_weight, down_weight):
    mine, width = rows_in.shape
    hidden = gate_weight.shape[1]
    out_width = down_weight.shape[1]
    rows = mine * hidden_size
    X = embed // 2
    A = 4 if hidden_size % 4 == 0 else 1
    B = hidden_size // A
    C = 7
    fc = hidden // C
    N = out_width // fc
    S, G, E, D = 12, 4, C - 3, 3
    dma = pltpu.SemaphoreType.DMA
    flops = 2 * rows * hidden * (2 * width + out_width)
    weights = 2 * hidden * (2 * width + out_width)
    half, rb = rows // 2, rows // embed
    return pl.pallas_call(
        functools.partial(kernel, (X, A, B, C, N, fc, S, G, E, D)),
        out_shape=jax.ShapeDtypeStruct((mine, out_width), BF16),
        in_specs=[pl.BlockSpec(memory_space=pl.ANY)] * 4,
        out_specs=pl.BlockSpec(memory_space=pltpu.VMEM),
        scratch_shapes=[
            pltpu.VMEM((rows, width), BF16),
            pltpu.VMEM((S, max(width, hidden), fc), BF16),
            pltpu.VMEM((C, rows, 2 * fc), F32),
            pltpu.VMEM((C, half, 2 * fc), F32),
            pltpu.VMEM((C, X - 1, rb, 2 * fc), BF16),
            pltpu.VMEM((C, X - 1, rb, 2 * fc), BF16),
            pltpu.VMEM((rows, hidden), BF16),
            pltpu.VMEM((N, rows, fc), F32),
            pltpu.VMEM((N, B, A * mine, fc), BF16),
            pltpu.VMEM((N, B - 1, A * mine, fc), BF16),
            pltpu.VMEM((N, A - 1, mine, fc), BF16),
            pltpu.VMEM((N, A - 1, mine, fc), BF16),
            dma((S,)), dma(()), dma((2, A)), dma((2, A, B)), dma((2, hidden_size)),
            dma((C,)), dma((C,)), dma((C, X - 1)), dma((C, X - 1)),
            dma((C, X - 1)), dma((C, X - 1)), dma((C,)), dma((C,)),
            dma((N, B - 1)), dma((N, B - 1)), dma((N, A - 1)), dma((N, A - 1)),
        ],
        compiler_params=pltpu.CompilerParams(
            collective_id=0, has_side_effects=True, vmem_limit_bytes=63 * 2**20
        ),
        cost_estimate=pl.CostEstimate(
            flops=flops, bytes_accessed=weights, transcendentals=rows * hidden // embed),
    )(rows_in, gate_weight, up_weight, down_weight)


def solution(mesh):
    placed = (
        P("hidden", "embed"),
        P("embed", "hidden"),
        P("embed", "hidden"),
        P("hidden", "embed"),
    )
    body = functools.partial(on_device, mesh.shape["embed"], mesh.shape["hidden"])
    return jax.shard_map(
        body, mesh=mesh, in_specs=placed, out_specs=P("hidden", "embed"), check_vma=False
    )
```

```python
import functools

import jax
import jax.numpy as jnp
from jax import lax
from jax.experimental import pallas as pl
from jax.experimental.pallas import tpu as pltpu
from jax.sharding import PartitionSpec as P

MESH = pl.DeviceIdType.MESH
F32 = jnp.float32
BF16 = jnp.bfloat16


def kernel(
    sizes, x_ref, gate_ref, up_ref, down_ref, out_ref,
    xg, wbuf, gu, l1r, l2s, l2r, act, yf, bs, br, zs, zr,
    wsem, own_sem, xa_s, xb_s, x_r, l1_ss, l1_rs, l2_ss, l2_rs,
    ax_ss, ax_rs, ac_ss, ac_rs, b_ss, b_rs, z_ss, z_rs,
):
    X, A, B, C, N, fc, S, G, E, D = sizes
    mine = x_ref.shape[0]
    rows, width = xg.shape
    hidden = act.shape[1]
    half = rows // 2
    rb = half // X
    e, h = lax.axis_index("embed"), lax.axis_index("hidden")
    x, c = e // 2, e % 2
    a, b = h // B, h % B
    half0 = pl.multiple_of(c * half, half)
    other0 = pl.multiple_of((1 - c) * half, half)
    own0 = pl.multiple_of(c * half + x * rb, rb)

    def at_embed(xx, cc):
        return {"embed": xx * 2 + cc, "hidden": h}

    def at_hidden(aa, bb):
        return {"embed": e, "hidden": aa * B + bb}

    def remote(src, dst, send, recv, where):
        return pltpu.make_async_remote_copy(
            src_ref=src, dst_ref=dst, send_sem=send, recv_sem=recv,
            device_id=where, device_id_type=MESH,
        )

    def cols(i):
        return pl.ds(pl.multiple_of(i * fc, fc), fc)

    def gate_tile(i, slot):
        return pltpu.make_async_copy(gate_ref.at[:, cols(i)], wbuf.at[slot, pl.ds(0, width), :], wsem.at[slot])

    def up_tile(i, slot):
        return pltpu.make_async_copy(up_ref.at[:, cols(i)], wbuf.at[slot, pl.ds(0, width), :], wsem.at[slot])

    def down_tile(j, slot):
        return pltpu.make_async_copy(down_ref.at[:, cols(j)], wbuf.at[slot, pl.ds(0, hidden), :], wsem.at[slot])

    def first_tiles(begin, end):
        for t in range(begin, end):
            (gate_tile if t % 2 == 0 else up_tile)(t // 2, t).start()

    first_tiles(0, 4)

    def block(hh):
        return xg.at[pl.ds(pl.multiple_of(hh * mine, mine), mine), :]

    own = pltpu.make_async_copy(x_ref, block(h), own_sem)
    own.start()

    barrier = pltpu.get_barrier_semaphore()
    peers = [at_embed((x + k) % X, c) for k in range(1, X)] + [at_embed(x, 1 - c)]
    peers += [at_hidden((a + k) % A, b) for k in range(1, A)]
    peers += [at_hidden(a, (b + k) % B) for k in range(1, B)]
    for where in peers:
        pl.semaphore_signal(barrier, inc=1, device_id=where, device_id_type=MESH)
    pl.semaphore_wait(barrier, len(peers))

    part = width // 2

    def piece(ref, q):
        return ref.at[:, pl.ds(q * part, part)]

    def x_outer(k, q):
        return remote(
            piece(x_ref, q), piece(block(h), q), xa_s.at[q, k], x_r.at[q, h], at_hidden((a + k) % A, b))

    def x_inner(k, m, q):
        hh = ((a - k + A) % A) * B + b
        src = block(hh) if not isinstance(k, int) or k > 0 else x_ref
        return remote(
            piece(src, q), piece(block(hh), q), xb_s.at[q, k, m], x_r.at[q, hh], at_hidden(a, (b + m) % B))

    def x_arrived(hh, q):
        there = piece(block(hh), q)
        remote(there, there, xa_s.at[q, 0], x_r.at[q, hh], at_hidden(a, b)).wait_recv()

    def x_forward(k, q):
        x_arrived(((a - k + A) % A) * B + b, q)
        for m in range(1, B):
            x_inner(k, m, q).start()

    def x_rest(q):
        for k in range(A):
            for m in range(1, B):
                x_arrived(((a - k + A) % A) * B + (b + m) % B, q)

    for q in range(2):
        for k in range(1, A):
            x_outer(k, q).start()
        for m in range(1, B):
            x_inner(0, m, q).start()
    first_tiles(4, S)
    for k in range(1, A):
        x_forward(k, 0)
    own.wait()
    x_rest(0)

    def early_step(i, _):
        for n, tile in ((0, gate_tile), (1, up_tile)):
            tile(i, 2 * i + n).wait()
            gu[i, :, pl.ds(n * fc, fc)] = jnp.dot(
                xg[:, pl.ds(0, part)], wbuf[2 * i + n, pl.ds(0, part), :], preferred_element_type=F32)

        @pl.when(i < A - 1)
        def _():
            x_forward(i + 1, 1)

        return 0

    lax.fori_loop(0, G, early_step, 0)
    x_rest(1)

    def l1(i):
        return remote(
            gu.at[i, pl.ds(other0, half), :], l1r.at[i], l1_ss.at[i], l1_rs.at[i], at_embed(x, 1 - c))

    def l2(i, k):
        return remote(
            l2s.at[i, k - 1], l2r.at[i, k - 1], l2_ss.at[i, k - 1], l2_rs.at[i, k - 1],
            at_embed((x + k) % X, c))

    def ax(i, k):
        part = act.at[pl.ds(own0, rb), cols(i)]
        return remote(part, part, ax_ss.at[i, k - 1], ax_rs.at[i, k - 1], at_embed((x + k) % X, c))

    def ax_in(i, k):
        xx = (x - k + X) % X
        part = act.at[pl.ds(pl.multiple_of(c * half + xx * rb, rb), rb), cols(i)]
        return remote(part, part, ax_ss.at[i, k - 1], ax_rs.at[i, k - 1], at_embed(x, c))

    def ac(i):
        part = act.at[pl.ds(half0, half), cols(i)]
        return remote(part, part, ac_ss.at[i], ac_rs.at[i], at_embed(x, 1 - c))

    def ac_in(i):
        part = act.at[pl.ds(other0, half), cols(i)]
        return remote(part, part, ac_ss.at[i], ac_rs.at[i], at_embed(x, c))

    def hidden_step(i, _):
        @pl.when(i < G)
        def _():
            for n in range(2):
                gu[i, :, pl.ds(n * fc, fc)] += jnp.dot(
                    xg[:, pl.ds(part, part)], wbuf[(2 * i + n) % S, pl.ds(part, part), :],
                    preferred_element_type=F32)

        @pl.when((i >= G) & (i < C))
        def _():
            for n, tile in ((0, gate_tile), (1, up_tile)):
                slot = (2 * i + n) % S
                tile(i, slot).wait()
                gu[i, :, pl.ds(n * fc, fc)] = jnp.dot(
                    xg[...], wbuf[slot, pl.ds(0, width), :], preferred_element_type=F32)

        @pl.when(i < C)
        def _():
            s0 = (2 * i) % S
            s1 = s0 + 1
            l1(i).start()
            t = 2 * i + S

            @pl.when(t < 2 * C)
            def _():
                gate_tile(t // 2, s0).start()
                up_tile(t // 2, s1).start()

            @pl.when((t >= 2 * C) & (t - 2 * C < N))
            def _():
                down_tile(t - 2 * C, s0).start()

            @pl.when((t >= 2 * C) & (t + 1 - 2 * C < N))
            def _():
                down_tile(t + 1 - 2 * C, s1).start()

        @pl.when((i >= 1) & (i < C + 1))
        def _():
            j = i - 1
            l1(j).wait_recv()
            for k in range(1, X):
                xx = (x + k) % X
                there = pl.ds(pl.multiple_of(xx * rb, rb), rb)
                here = pl.ds(pl.multiple_of(c * half + xx * rb, rb), rb)
                l2s[j, k - 1] = (gu[j, here, :] + l1r[j, there, :]).astype(BF16)
                l2(j, k).start()

        @pl.when((i >= 3) & (i < C + 3))
        def _():
            j = i - 3
            total = gu[j, pl.ds(own0, rb), :] + l1r[j, pl.ds(pl.multiple_of(x * rb, rb), rb), :]
            for k in range(1, X):
                l2(j, k).wait_recv()
                total = total + l2r[j, k - 1].astype(F32)
            g, u = total[:, :fc], total[:, fc:]
            act[pl.ds(own0, rb), cols(j)] = (g / (1.0 + jnp.exp(-g)) * u).astype(BF16)
            for k in range(1, X):
                ax(j, k).start()

        @pl.when(i >= 5)
        def _():
            j = i - 5
            for k in range(1, X):
                ax_in(j, k).wait_recv()
            ac(j).start()

        @pl.when(i == C + 5 - D)
        def _():
            for j in range(E):
                ac_in(j).wait_recv()

        @pl.when(i >= C + 5 - D)
        def _():
            j = i - (C + 5 - D)
            slot = (2 * C + j) % S
            down_tile(j, slot).wait()
            yf[j] = jnp.dot(
                act[:, pl.ds(0, E * fc)], wbuf[slot, pl.ds(0, E * fc), :], preferred_element_type=F32)

        return 0

    lax.fori_loop(0, C + 5, hidden_step, 0)

    def act_in(i, _):
        ac_in(i).wait_recv()
        return 0

    lax.fori_loop(E, C, act_in, 0)

    def sb(j, m):
        return remote(
            bs.at[j, (b + m) % B], br.at[j, m - 1], b_ss.at[j, m - 1], b_rs.at[j, m - 1],
            at_hidden(a, (b + m) % B))

    def sz(j, k):
        return remote(
            zs.at[j, k - 1], zr.at[j, k - 1], z_ss.at[j, k - 1], z_rs.at[j, k - 1],
            at_hidden((a + k) % A, b))

    def inner_sum(j, aa):
        s = yf[j, pl.ds(pl.multiple_of((aa * B + b) * mine, mine), mine), :]
        for m in range(1, B):
            s = s + br[j, m - 1, pl.ds(pl.multiple_of(aa * mine, mine), mine), :].astype(F32)
        return s

    def out_step(i, _):
        slot = (2 * C + i) % S
        late = pl.ds(E * fc, hidden - E * fc)

        @pl.when(i < D)
        def _():
            yf[i] += jnp.dot(act[:, late], wbuf[slot, late, :], preferred_element_type=F32)

        @pl.when((i >= D) & (i < N))
        def _():
            down_tile(i, slot).wait()
            yf[i] = jnp.dot(act[...], wbuf[slot, pl.ds(0, hidden), :], preferred_element_type=F32)

        @pl.when(i < N)
        def _():
            for aa in range(A):
                for bb in range(B):
                    bs[i, bb, pl.ds(aa * mine, mine), :] = yf[
                        i, pl.ds((aa * B + bb) * mine, mine), :].astype(BF16)
            for m in range(1, B):
                sb(i, m).start()

            @pl.when(i + S < N)
            def _():
                down_tile(i + S, slot).start()

        @pl.when((i >= 2) & (i < N + 2))
        def _():
            j = i - 2
            for m in range(1, B):
                sb(j, m).wait_recv()
            for k in range(1, A):
                zs[j, k - 1] = inner_sum(j, (a + k) % A).astype(BF16)
                sz(j, k).start()

        @pl.when(i >= 4)
        def _():
            j = i - 4
            s = inner_sum(j, a)
            for k in range(1, A):
                sz(j, k).wait_recv()
                s = s + zr[j, k - 1].astype(F32)
            out_ref[:, cols(j)] = s.astype(BF16)

        return 0

    lax.fori_loop(0, N + 4, out_step, 0)

    for q in range(2):
        for k in range(1, A):
            x_outer(k, q).wait_send()
        for k in range(A):
            for m in range(1, B):
                x_inner(k, m, q).wait_send()

    def hidden_sent(i, _):
        l1(i).wait_send()
        for k in range(1, X):
            l2(i, k).wait_send()
            ax(i, k).wait_send()
        ac(i).wait_send()
        return 0

    lax.fori_loop(0, C, hidden_sent, 0)

    def out_sent(j, _):
        for m in range(1, B):
            sb(j, m).wait_send()
        for k in range(1, A):
            sz(j, k).wait_send()
        return 0

    lax.fori_loop(0, N, out_sent, 0)


def on_device(embed, hidden_size, rows_in, gate_weight, up_weight, down_weight):
    mine, width = rows_in.shape
    hidden = gate_weight.shape[1]
    out_width = down_weight.shape[1]
    rows = mine * hidden_size
    X = embed // 2
    A = 4 if hidden_size % 4 == 0 else 1
    B = hidden_size // A
    C = 7
    fc = hidden // C
    N = out_width // fc
    S, G, E, D = 12, 4, C - 3, 3
    dma = pltpu.SemaphoreType.DMA
    flops = 2 * rows * hidden * (2 * width + out_width)
    weights = 2 * hidden * (2 * width + out_width)
    half, rb = rows // 2, rows // embed
    return pl.pallas_call(
        functools.partial(kernel, (X, A, B, C, N, fc, S, G, E, D)),
        out_shape=jax.ShapeDtypeStruct((mine, out_width), BF16),
        in_specs=[pl.BlockSpec(memory_space=pl.ANY)] * 4,
        out_specs=pl.BlockSpec(memory_space=pltpu.VMEM),
        scratch_shapes=[
            pltpu.VMEM((rows, width), BF16),
            pltpu.VMEM((S, max(width, hidden), fc), BF16),
            pltpu.VMEM((C, rows, 2 * fc), F32),
            pltpu.VMEM((C, half, 2 * fc), F32),
            pltpu.VMEM((C, X - 1, rb, 2 * fc), BF16),
            pltpu.VMEM((C, X - 1, rb, 2 * fc), BF16),
            pltpu.VMEM((rows, hidden), BF16),
            pltpu.VMEM((N, rows, fc), F32),
            pltpu.VMEM((N, B, A * mine, fc), BF16),
            pltpu.VMEM((N, B - 1, A * mine, fc), BF16),
            pltpu.VMEM((N, A - 1, mine, fc), BF16),
            pltpu.VMEM((N, A - 1, mine, fc), BF16),
            dma((S,)), dma(()), dma((2, A)), dma((2, A, B)), dma((2, hidden_size)),
            dma((C,)), dma((C,)), dma((C, X - 1)), dma((C, X - 1)),
            dma((C, X - 1)), dma((C, X - 1)), dma((C,)), dma((C,)),
            dma((N, B - 1)), dma((N, B - 1)), dma((N, A - 1)), dma((N, A - 1)),
        ],
        compiler_params=pltpu.CompilerParams(
            collective_id=0, has_side_effects=True, vmem_limit_bytes=63 * 2**20
        ),
        cost_estimate=pl.CostEstimate(
            flops=flops, bytes_accessed=weights, transcendentals=rows * hidden // embed),
    )(rows_in, gate_weight, up_weight, down_weight)


def solution(mesh):
    placed = (
        P("hidden", "embed"),
        P("embed", "hidden"),
        P("embed", "hidden"),
        P("hidden", "embed"),
    )
    body = functools.partial(on_device, mesh.shape["embed"], mesh.shape["hidden"])
    return jax.shard_map(
        body, mesh=mesh, in_specs=placed, out_specs=P("hidden", "embed"), check_vma=False
    )
```
